32 devices in a mesh: prow: 4 (over z), pcol: 8 (over y, x, core).
Axes of the slice: x: 2, y: 2, z: 4, core: 2. Of those that a mesh axis runs over, the one named last changes fastest.
Arguments:
- eigvecs: float32 [16384, 2048], P(('prow', 'pcol')), may hold values from -6 to 6
- bulge_vectors: float32 [4, 16384], replicated, may hold values from -2 to 2, as said below
- panel_vectors: float32 [2, 16384, 256], P(None, 'prow'), may hold values from -0.046875 to 0.046875
- panel_factor: float32 [2, 256, 256], replicated, may hold values from -0.5 to 2, as said below
Outputs:
- back_vectors: float32 [16384, 2048], P('prow', 'pcol')
The draws below stay inside these ranges and needn't reach their ends.
Inputs may be any that keep to these rules, and one draw needn't show every extreme that they name: `bulge_vectors`: every entry has magnitude between 0.25 and 2. `panel_factor`: each factor is upper triangular; its diagonal lies between 1 and 2.
All inputs are finite; a program needn't handle non-finite values.
Results may differ from the reference program's by a relative error of at most 0.0003.
Values sent between devices are 32-bit elements; how exact they have to be, the bound alone decides.
A program may use at most 128 MiB of HBM per device.

```python
import jax
import jax.numpy as jnp
from jax import lax

BAND = 128
SWEEPS = 4
MODES = 2048
PANEL = 256
PANELS = 2
ORDER = 16384


def draw_bulge_vectors(key, part):
    key = jax.random.fold_in(key, 11)
    first, second = jax.random.split(key)
    shape = (SWEEPS, ORDER)
    signs = jnp.where(jax.random.bernoulli(first, 0.5, shape), 1.0, -1.0)
    sizes = jax.random.uniform(second, shape, jnp.float32, 0.5, 1.5)
    return (signs * sizes).astype(jnp.float32)


def draw_panel_factor(key, part):
    key = jax.random.fold_in(key, 23)
    first, second = jax.random.split(key)
    shape = (PANELS, PANEL, PANEL)
    upper = jnp.clip(0.08 * jax.random.normal(first, shape, jnp.float32), -0.5, 0.5)
    diag = jax.random.uniform(second, shape, jnp.float32, 1.0, 2.0)
    row_ids = lax.broadcasted_iota(jnp.int32, shape, 1)
    col_ids = lax.broadcasted_iota(jnp.int32, shape, 2)
    full = jnp.where(row_ids < col_ids, upper, jnp.where(row_ids == col_ids, diag, 0.0))
    return full.astype(jnp.float32)


def shard_levels(own_key, extent, cuts, low, top_value):
    level = 1.0
    for dim, blocks in cuts:
        heights = jax.random.uniform(jax.random.fold_in(jax.random.fold_in(own_key, 6), dim), (blocks,), jnp.float32, low / len(cuts), top_value / len(cuts))
        level = level * jnp.repeat(jnp.exp(heights), extent[dim] // blocks).reshape((-1,) + (1,) * (len(extent) - 1 - dim))
    return level


def bell_draw(stream_key, dims, scale, limit, cuts=(), held_as=jnp.bfloat16):
    values = scale * jax.random.normal(stream_key, dims, jnp.float32)
    if cuts:
        values = values * shard_levels(stream_key, dims, cuts, -0.22, 0.18)
    return jnp.clip(values, -limit, limit).astype(held_as)


def setup_inputs(seed: int = 0) -> dict:
    splits = jax.random.split(jax.random.key(seed), 5)
    return {
        "eigvecs": bell_draw(splits[0], (ORDER, MODES), 1.0, 6.0, ((0, 32),), jnp.float32),
        "bulge_vectors": draw_bulge_vectors(jax.random.fold_in(splits[4], 71), 0),
        "panel_vectors": bell_draw(splits[2], (PANELS, ORDER, PANEL), ORDER ** -0.5, 0.046875, ((1, 4),), jnp.float32),
        "panel_factor": draw_panel_factor(jax.random.fold_in(splits[4], 71), 0),
    }


def apply_sweep(field, vectors, offset, band):
    if offset:
        field = jnp.pad(field, ((band - offset, offset), (0, 0)))
        vectors = jnp.pad(vectors, (band - offset, offset))
    length = field.shape[0]
    blocks = field.reshape(length // band, band, field.shape[1])
    pieces = vectors.reshape(length // band, band)
    norms = jnp.sum(pieces * pieces, axis=1)
    positive = norms > 0
    scales = jnp.where(positive, 2.0 / jnp.where(positive, norms, 1.0), 0.0)
    weights = jnp.einsum("br,brm->bm", pieces, blocks, precision=lax.Precision.HIGHEST)
    blocks = blocks - (scales[:, None] * pieces)[:, :, None] * weights[:, None, :]
    field = blocks.reshape(length, field.shape[1])
    if offset:
        field = field[band - offset:length - offset]
    return field


def reference(eigvecs, bulge_vectors, panel_vectors, panel_factor):
    field = eigvecs
    for sweep in range(SWEEPS):
        field = apply_sweep(field, bulge_vectors[sweep], sweep * BAND // SWEEPS, BAND)
    for panel in range(PANELS):
        proj = jnp.dot(panel_vectors[panel].T, field, precision=lax.Precision.HIGHEST, preferred_element_type=jnp.float32)
        mixed = jnp.dot(panel_factor[panel], proj, precision=lax.Precision.HIGHEST, preferred_element_type=jnp.float32)
        field = field - jnp.dot(panel_vectors[panel], mixed, precision=lax.Precision.HIGHEST, preferred_element_type=jnp.float32)
    return field
```

```python
import jax
import jax.numpy as jnp
from jax import lax
from jax.sharding import PartitionSpec as P

BAND = 128


def apply_blocks(field, vectors, start, band):
    length = (field.shape[0] - start) // band * band
    part = field[start : start + length]
    blocks = part.reshape(length // band, band, field.shape[1])
    pieces = vectors[start : start + length].reshape(length // band, band)
    norms = jnp.sum(pieces * pieces, axis=1)
    positive = norms > 0
    scales = jnp.where(positive, 2.0 / jnp.where(positive, norms, 1.0), 0.0)
    weights = jnp.sum(pieces[:, :, None] * blocks, axis=1)
    blocks = blocks - (scales[:, None] * pieces)[:, :, None] * weights[:, None, :]
    return jnp.concatenate(
        [field[:start], blocks.reshape(length, field.shape[1]), field[start + length :]]
    )


def project(vectors, field):
    return lax.dot_general(
        vectors,
        field,
        (((0,), (0,)), ((), ())),
        precision=lax.Precision.HIGHEST,
        preferred_element_type=jnp.float32,
    )


def product(left, right):
    return jnp.dot(left, right, precision=lax.Precision.HIGHEST, preferred_element_type=jnp.float32)


def local(eigvecs, bulge_vectors, panel_vectors, panel_factor):
    sweeps = bulge_vectors.shape[0]
    band = BAND
    field = lax.all_to_all(eigvecs, "pcol", split_axis=1, concat_axis=0, tiled=True)
    rows = field.shape[0]
    peers = lax.axis_size("prow")
    up = [(i, i + 1) for i in range(peers - 1)]
    down = [(i + 1, i) for i in range(peers - 1)]
    before = lax.ppermute(field[rows - band :], "prow", up)
    after = lax.ppermute(field[: 3 * band], "prow", down)
    extended = jnp.concatenate([before, field, after])
    first_row = lax.axis_index("prow") * rows
    padded = jnp.pad(bulge_vectors, ((0, 0), (band, 3 * band)))
    vectors = lax.dynamic_slice_in_dim(padded, first_row, rows + 4 * band, 1)
    for sweep in range(sweeps):
        extended = apply_blocks(extended, vectors[sweep], sweep * band // sweeps, band)
    field = extended[band : band + rows]
    p1 = project(panel_vectors[0], field)
    p2 = project(panel_vectors[1], field)
    g = project(panel_vectors[1], panel_vectors[0])
    p1, p2, g = lax.psum((p1, p2, g), "prow")
    m1 = product(panel_factor[0], p1)
    m2 = product(panel_factor[1], p2 - product(g, m1))
    both = jnp.concatenate([panel_vectors[0], panel_vectors[1]], axis=1)
    return field - product(both, jnp.concatenate([m1, m2]))


def solution(mesh):
    placed = (P(("prow", "pcol"), None), P(), P(None, "prow", None), P())
    return jax.shard_map(
        local, mesh=mesh, in_specs=placed, out_specs=P("prow", "pcol"), check_vma=False
    )
```

```python
import functools

import jax
import jax.numpy as jnp
from jax import lax
from jax.experimental import pallas as pl
from jax.experimental.pallas import tpu as pltpu
from jax.sharding import PartitionSpec as P

BAND = 128
LANES = 128
MESH = pl.DeviceIdType.MESH
F32 = jnp.float32
BF16 = jnp.bfloat16
HIGHEST = lax.Precision.HIGHEST


def split(x):
    high = x.astype(BF16)
    return high, (x - high.astype(F32)).astype(BF16)


def dot(a, b):
    return jnp.dot(a, b, preferred_element_type=F32)


def kernel(
    nrow, ncol, sweeps, eig, refl, panels, factor, out,
    field, spread, vecs, vt_hi, vt_lo, acc, part, gather, total, mixw,
    load_sem, self_sem, send_sem, recv_sem, halo_send, halo_recv,
    rs_send, rs_recv, ag_send, ag_recv, out_sem,
):
    prow, pcol = lax.axis_index("prow"), lax.axis_index("pcol")
    block = eig.shape[0]
    chunks = field.shape[0]
    rows = block * ncol
    count = rows // BAND
    step = BAND // sweeps
    edge = BAND - step
    rank = panels.shape[2]
    width = 2 * rank
    piece = width // nrow
    tile = 512
    tiles = rows // tile

    vec_load = pltpu.make_async_copy(panels, vecs, load_sem)
    vec_load.start()

    barrier = pltpu.get_barrier_semaphore()
    for off in range(1, ncol):
        pl.semaphore_signal(barrier, inc=1, device_id=(prow, lax.rem(pcol + off, ncol)), device_id_type=MESH)
    for off in range(1, nrow):
        pl.semaphore_signal(barrier, inc=1, device_id=(lax.rem(prow + off, nrow), pcol), device_id_type=MESH)
    pl.semaphore_wait(barrier, ncol + nrow - 2)

    def exchange(k, off):
        peer = lax.rem(pcol + off, ncol)
        cols = pl.ds(pl.multiple_of(peer * (chunks * LANES) + k * LANES, LANES), LANES)
        return pltpu.make_async_remote_copy(
            src_ref=eig.at[:, cols],
            dst_ref=field.at[k, pl.ds(pl.multiple_of(BAND + pcol * block, BAND), block), :],
            send_sem=send_sem.at[k, off],
            recv_sem=recv_sem.at[k, pcol],
            device_id=(prow, peer),
            device_id_type=MESH,
        )

    def arrival(k, off):
        peer = lax.rem(pcol + ncol - off, ncol)
        return pltpu.make_async_remote_copy(
            src_ref=eig.at[:, pl.ds(0, LANES)],
            dst_ref=field.at[k, pl.ds(pl.multiple_of(BAND + peer * block, BAND), block), :],
            send_sem=send_sem.at[k, off],
            recv_sem=recv_sem.at[k, peer],
            device_id=(prow, peer),
            device_id_type=MESH,
        )

    def own(k):
        cols = pl.ds(pl.multiple_of(pcol * (chunks * LANES) + k * LANES, LANES), LANES)
        return pltpu.make_async_copy(
            eig.at[:, cols],
            field.at[k, pl.ds(pl.multiple_of(BAND + pcol * block, BAND), block), :],
            self_sem.at[k],
        )

    for k in range(chunks):
        for off in range(1, ncol):
            exchange(k, off).start()
        own(k).start()

    for k in range(chunks):
        @pl.when(prow == 0)
        def _():
            field[k, pl.ds(0, BAND), :] = jnp.zeros((BAND, LANES), F32)

        @pl.when(prow == nrow - 1)
        def _():
            field[k, pl.ds(BAND + rows, BAND), :] = jnp.zeros((BAND, LANES), F32)

    def reduce_copy(idx, off):
        peer = lax.rem(prow + off, nrow)
        return pltpu.make_async_remote_copy(
            src_ref=part.at[idx, pl.ds(pl.multiple_of(peer * piece, piece), piece), :],
            dst_ref=gather.at[idx, prow],
            send_sem=rs_send.at[idx, off],
            recv_sem=rs_recv.at[idx, prow],
            device_id=(peer, pcol),
            device_id_type=MESH,
        )

    def reduce_arrival(idx, off):
        peer = lax.rem(prow + nrow - off, nrow)
        return pltpu.make_async_remote_copy(
            src_ref=part.at[idx, pl.ds(0, piece), :],
            dst_ref=gather.at[idx, peer],
            send_sem=rs_send.at[idx, off],
            recv_sem=rs_recv.at[idx, peer],
            device_id=(peer, pcol),
            device_id_type=MESH,
        )

    def share_copy(idx, off):
        peer = lax.rem(prow + off, nrow)
        mine = pl.ds(pl.multiple_of(prow * piece, piece), piece)
        return pltpu.make_async_remote_copy(
            src_ref=total.at[idx, mine, :],
            dst_ref=total.at[idx, mine, :],
            send_sem=ag_send.at[idx, off],
            recv_sem=ag_recv.at[idx, prow],
            device_id=(peer, pcol),
            device_id_type=MESH,
        )

    def share_arrival(idx, off):
        peer = lax.rem(prow + nrow - off, nrow)
        theirs = pl.ds(pl.multiple_of(peer * piece, piece), piece)
        return pltpu.make_async_remote_copy(
            src_ref=total.at[idx, theirs, :],
            dst_ref=total.at[idx, theirs, :],
            send_sem=ag_send.at[idx, off],
            recv_sem=ag_recv.at[idx, peer],
            device_id=(peer, pcol),
            device_id_type=MESH,
        )

    def reduce_start(idx):
        for off in range(1, nrow):
            reduce_copy(idx, off).start()

    def reduce_end(idx):
        mine = pl.ds(pl.multiple_of(prow * piece, piece), piece)
        value = part[idx, mine, :]
        for off in range(1, nrow):
            reduce_arrival(idx, off).wait_recv()
            value = value + gather[idx, lax.rem(prow + nrow - off, nrow)]
        total[idx, mine, :] = value
        for off in range(1, nrow):
            share_copy(idx, off).start()

    def share_end(idx):
        for off in range(1, nrow):
            share_arrival(idx, off).wait_recv()

    vec_load.wait()

    def turn(t, carry):
        at = pl.multiple_of(t * 256, 256)
        for p in range(2):
            high, low = split(vecs[p, pl.ds(at, 256), :].T)
            vt_hi[pl.ds(p * rank, rank), pl.ds(at, 256)] = high
            vt_lo[pl.ds(p * rank, rank), pl.ds(at, 256)] = low
        return carry

    lax.fori_loop(0, rows // 256, turn, 0)

    acc[...] = jnp.zeros_like(acc)

    def cross(t, carry):
        at = pl.multiple_of(t * tile, tile)
        high, low = split(vecs[0, pl.ds(at, tile), :])
        left = vt_hi[pl.ds(rank, rank), pl.ds(at, tile)]
        acc[pl.ds(0, rank), :] += (
            dot(left, high) + dot(left, low) + dot(vt_lo[pl.ds(rank, rank), pl.ds(at, tile)], high)
        )
        return carry

    lax.fori_loop(0, tiles, cross, 0)
    part[chunks, pl.ds(0, rank), :] = acc[pl.ds(0, rank), pl.ds(0, LANES)]
    part[chunks, pl.ds(rank, rank), :] = acc[pl.ds(0, rank), pl.ds(LANES, LANES)]
    reduce_start(chunks)

    def spread_sweep(s):
        def body(j, carry):
            row = refl[s * (count + 1) + j]
            spread[s, pl.ds(pl.multiple_of(j * BAND, BAND), BAND), :] = jnp.broadcast_to(row, (BAND, BAND)).T
            return carry

        lax.fori_loop(0, count + 1, body, 0)

    spread_sweep(0)
    spread_sweep(1)
    reduce_end(chunks)
    for s in range(2, sweeps):
        spread_sweep(s)
    share_end(chunks)
    cross_full = jnp.concatenate([total[chunks, pl.ds(0, rank), :], total[chunks, pl.ds(rank, rank), :]], axis=1)
    right = jnp.dot(cross_full, factor[0], precision=HIGHEST, preferred_element_type=F32)
    mixw[...] = jnp.dot(factor[1], right, precision=HIGHEST, preferred_element_type=F32)

    def reflect(k, s, j):
        at = pl.multiple_of(s * step + j * BAND, 8)
        u = spread[s, pl.ds(pl.multiple_of(j * BAND, BAND), BAND), :]
        f = field[k, pl.ds(at, BAND), :]
        w = jnp.sum(u * f, axis=0, keepdims=True)
        field[k, pl.ds(at, BAND), :] = f - u * w

    def run(k, s, first, last):
        group = 4
        full = (last - first) // group

        def body(i, carry):
            for g in range(group):
                reflect(k, s, first + i * group + g)
            return carry

        lax.fori_loop(0, full, body, 0)
        for j in range(first + full * group, last):
            reflect(k, s, j)

    def halo(k, side):
        if side == 0:
            src, dst, peer = BAND, BAND + rows, prow - 1
        else:
            src, dst, peer = BAND + rows - edge, BAND - edge, prow + 1
        return pltpu.make_async_remote_copy(
            src_ref=field.at[k, pl.ds(src, edge), :],
            dst_ref=field.at[k, pl.ds(dst, edge), :],
            send_sem=halo_send.at[k, side],
            recv_sem=halo_recv.at[k, side],
            device_id=(peer, pcol),
            device_id_type=MESH,
        )

    def sweep_all(k):
        run(k, 0, 1, count + 1)

        @pl.when(prow < nrow - 1)
        def _():
            halo(k, 1).start()

        for s in range(1, sweeps - 1):
            run(k, s, 1, count + 1 - s)

        @pl.when(prow > 0)
        def _():
            halo(k, 0).start()

        run(k, sweeps - 1, 1, count + 2 - sweeps)

        @pl.when(prow < nrow - 1)
        def _():
            halo(k, 1).wait_send()
            halo(k, 0).wait_recv()

        @pl.when(prow > 0)
        def _():
            halo(k, 0).wait_send()
            halo(k, 1).wait_recv()

        for s in range(1, sweeps):
            reflect(k, s, 0)
            for j in range(count + 1 - s, count + 1):
                reflect(k, s, j)

    def project(k):
        acc[...] = jnp.zeros_like(acc)

        def body(t, carry):
            at = pl.multiple_of(t * tile, tile)
            high, low = split(field[k, pl.ds(pl.multiple_of(BAND + at, BAND), tile), :])
            right = jnp.concatenate([high, low], axis=1)
            acc[...] += dot(vt_hi[:, pl.ds(at, tile)], right)
            acc[:, pl.ds(0, LANES)] += dot(vt_lo[:, pl.ds(at, tile)], high)
            return carry

        lax.fori_loop(0, tiles, body, 0)
        part[k] = acc[:, pl.ds(0, LANES)] + acc[:, pl.ds(LANES, LANES)]

    def out_copy(k, t):
        at = pl.multiple_of(t * tile, tile)
        return pltpu.make_async_copy(
            field.at[k, pl.ds(pl.multiple_of(BAND + at, BAND), tile), :],
            out.at[pl.ds(at, tile), pl.ds(k * LANES, LANES)],
            out_sem.at[k, t],
        )

    def update(k):
        first = total[k, pl.ds(0, rank), :]
        second = total[k, pl.ds(rank, rank), :]
        m1 = jnp.dot(factor[0], first, precision=HIGHEST, preferred_element_type=F32)
        m2 = jnp.dot(factor[1], second, precision=HIGHEST, preferred_element_type=F32)
        m2 = m2 - jnp.dot(mixw[...], first, precision=HIGHEST, preferred_element_type=F32)
        rights = []
        for m in (m1, m2):
            high, low = split(m)
            rights.append((high, jnp.concatenate([high, low], axis=1)))

        def body(t, carry):
            at = pl.multiple_of(t * tile, tile)
            for p in range(2):
                high, low = split(vecs[p, pl.ds(at, tile), :])
                both = dot(high, rights[p][1])
                rest = dot(low, rights[p][0])
                if p == 0:
                    change = both[:, :LANES] + both[:, LANES:] + rest
                else:
                    change = change + (both[:, :LANES] + both[:, LANES:] + rest)
            where = pl.ds(pl.multiple_of(BAND + at, BAND), tile)
            field[k, where, :] = field[k, where, :] - change
            out_copy(k, t).start()
            return carry

        lax.fori_loop(0, tiles, body, 0)

    for k in range(chunks):
        own(k).wait()
        for off in range(1, ncol):
            arrival(k, off).wait_recv()
        sweep_all(k)
        project(k)
        reduce_start(k)
        if k > 0:
            share_end(k - 1)
            update(k - 1)
        reduce_end(k)
    share_end(chunks - 1)
    update(chunks - 1)

    for k in range(chunks):
        for off in range(1, ncol):
            exchange(k, off).wait_send()
    for idx in range(chunks + 1):
        for off in range(1, nrow):
            reduce_copy(idx, off).wait_send()
            share_copy(idx, off).wait_send()
    for k in range(chunks):
        for t in range(tiles):
            out_copy(k, t).wait()


def local(eigvecs, bulge_vectors, panel_vectors, panel_factor):
    sweeps = bulge_vectors.shape[0]
    nrow, ncol = lax.axis_size("prow"), lax.axis_size("pcol")
    block, modes = eigvecs.shape
    columns = modes // ncol
    chunks = columns // LANES
    rows = block * ncol
    rank = panel_vectors.shape[2]
    width = 2 * rank
    piece = width // nrow
    count = rows // BAND
    tiles = rows // 512

    padded = jnp.pad(bulge_vectors, ((0, 0), (BAND, BAND)))
    window = lax.dynamic_slice_in_dim(padded, lax.axis_index("prow") * rows, rows + 2 * BAND, 1)
    shifted = jnp.stack(
        [window[s, s * BAND // sweeps : s * BAND // sweeps + rows + BAND] for s in range(sweeps)]
    ).reshape(sweeps * (count + 1), 1, BAND)
    norms = jnp.sum(shifted * shifted, axis=2, keepdims=True)
    positive = norms > 0
    shifted = shifted * jnp.where(positive, jnp.sqrt(2.0 / jnp.where(positive, norms, 1.0)), 0.0)

    dma = pltpu.SemaphoreType.DMA
    vmem = pl.BlockSpec(memory_space=pltpu.VMEM)
    hbm = pl.BlockSpec(memory_space=pl.ANY)
    return pl.pallas_call(
        functools.partial(kernel, nrow, ncol, sweeps),
        out_shape=jax.ShapeDtypeStruct((rows, columns), F32),
        in_specs=[hbm, vmem, hbm, vmem],
        out_specs=hbm,
        scratch_shapes=[
            pltpu.VMEM((chunks, rows + 2 * BAND, LANES), F32),
            pltpu.VMEM((sweeps, rows + BAND, BAND), F32),
            pltpu.VMEM((2, rows, rank), F32),
            pltpu.VMEM((width, rows), BF16),
            pltpu.VMEM((width, rows), BF16),
            pltpu.VMEM((width, 2 * LANES), F32),
            pltpu.VMEM((chunks + 1, width, LANES), F32),
            pltpu.VMEM((chunks + 1, nrow, piece, LANES), F32),
            pltpu.VMEM((chunks + 1, width, LANES), F32),
            pltpu.VMEM((rank, rank), F32),
            dma,
            dma((chunks,)),
            dma((chunks, ncol)),
            dma((chunks, ncol)),
            dma((chunks, 2)),
            dma((chunks, 2)),
            dma((chunks + 1, nrow)),
            dma((chunks + 1, nrow)),
            dma((chunks + 1, nrow)),
            dma((chunks + 1, nrow)),
            dma((chunks, tiles)),
        ],
        compiler_params=pltpu.CompilerParams(
            collective_id=0, has_side_effects=True, vmem_limit_bytes=62 * 1024 * 1024
        ),
        cost_estimate=pl.CostEstimate(
            flops=4 * rows * width * columns, bytes_accessed=16 * rows * columns, transcendentals=0
        ),
    )(eigvecs, shifted, panel_vectors, panel_factor)


def solution(mesh):
    placed = (P(("prow", "pcol"), None), P(), P(None, "prow", None), P())
    return jax.shard_map(
        local, mesh=mesh, in_specs=placed, out_specs=P("prow", "pcol"), check_vma=False
    )
```
